32 devices in a mesh: out: 16 (over z, y, x), con: 2 (over core).
Axes of the slice: x: 2, y: 2, z: 4, core: 2. Of those that a mesh axis runs over, the one named last changes fastest.
Arguments:
- amplitudes: bfloat16 [512, 9216], P(('out', 'con')), may hold values from -6 to 6
- integrals: bfloat16 [16384, 9216], P('out', 'con'), may hold values from -0.078125 to 0.078125
- block_sizes: int32 [8], replicated, may hold values from 64 to 192, as said below
Outputs:
- ladder: bfloat16 [512, 16384], P('con', 'out')
The draws below stay inside these ranges and needn't reach their ends.
Inputs may be any that keep to these rules, and one draw needn't show every extreme that they name: `block_sizes`: each entry lies between 64 and 192; the entries sum to 1024; one entry equals 192 and one equals 64.
All inputs are finite; a program needn't handle non-finite values.
Results may differ from the reference program's by a relative error of at most 0.001.
Values may be sent and summed in bfloat16 or wider, within the bound.
No kernel may reach another device: no remote copies, remote signals or barrier semaphores. Data moves between devices by JAX's collectives and lax.ppermute only.
A program may use at most 64 MiB of HBM per device.

```python
import jax
import jax.numpy as jnp
from jax import lax

NVIR = 1024
NIRREP = 8
DMAX = 192
CW = 6
OPAIRS = 512
ROWS_OUT = 1024
OUTP = 16384
NCOL = 9216
N_OUT = 16


def draw_block_sizes(key, part):
    first_key, second_key = jax.random.split(key)
    middle = NVIR // NIRREP
    lowest = 2 * middle - DMAX
    half_count = (NIRREP - 2) // 2
    deltas = jax.random.randint(first_key, (half_count,), lowest - middle, DMAX - middle + 1)
    values = jnp.concatenate([jnp.array([lowest, DMAX], dtype=jnp.int32), (middle + deltas).astype(jnp.int32), (middle - deltas).astype(jnp.int32)])
    order = jax.random.permutation(second_key, NIRREP)
    return values[order].astype(jnp.int32)


def levels(rng, shape, pieces, least, high):
    def one(dim, blocks):
        draws = jax.random.uniform(jax.random.fold_in(jax.random.fold_in(rng, 6), dim), (blocks,), jnp.float32, least / len(pieces), high / len(pieces))
        return jnp.repeat(jnp.exp(draws), shape[dim] // blocks).reshape((-1,) + (1,) * (len(shape) - dim - 1))

    level = one(*pieces[0])
    for cut in pieces[1:]:
        level = level * one(*cut)
    return level


def bell_draw(key, shape, spread, limit, pieces=(), kind=jnp.bfloat16):
    values = spread * jax.random.normal(key, shape, jnp.float32)
    if pieces:
        values = values * levels(key, shape, pieces, -0.22, 0.18)
    return jnp.clip(values, -limit, limit).astype(kind)


def setup_inputs(seed: int = 0) -> dict:
    arg_keys = jax.random.split(jax.random.key(seed), 4)
    amplitudes = bell_draw(arg_keys[0], (OPAIRS, NCOL), 1.0, 6.0, ((0, 32),))
    integrals = bell_draw(arg_keys[1], (OUTP, NCOL), (CW * NVIR) ** -0.5, 0.078125, ((0, 16), (1, 2)))
    block_sizes = draw_block_sizes(jax.random.fold_in(arg_keys[3], 71), 0)
    return {"amplitudes": amplitudes, "integrals": integrals, "block_sizes": block_sizes}


def reference(amplitudes, integrals, block_sizes):
    blocked = amplitudes.reshape(OPAIRS, NIRREP, CW, DMAX)
    valid_cols = jnp.arange(DMAX, dtype=jnp.int32)[None, :] < block_sizes[:, None]
    masked = jnp.where(valid_cols[None, :, None, :], blocked, jnp.zeros((), amplitudes.dtype))
    masked = masked.reshape(OPAIRS, NCOL).astype(jnp.float32)
    row_blocks = integrals.reshape(N_OUT, ROWS_OUT, NCOL)

    def one_block(row_block):
        return lax.dot_general(masked, row_block.astype(jnp.float32), (((1,), (1,)), ((), ())),
                               precision=lax.Precision.HIGHEST, preferred_element_type=jnp.float32)

    results = lax.map(one_block, row_blocks)
    ladder = jnp.transpose(results, (1, 0, 2)).reshape(OPAIRS, OUTP)
    return ladder.astype(jnp.bfloat16)
```

```python
import functools

import jax
import jax.numpy as jnp
from jax import lax
from jax.experimental import pallas as pl
from jax.experimental.pallas import tpu as pltpu
from jax.sharding import PartitionSpec as P

DMAX = 192
LANES = 128
LOW = 64
ROWS = 16


def mask_slots(amplitudes, block_sizes):
    row_count = amplitudes.shape[0]
    nirrep = block_sizes.shape[0]
    blocked = amplitudes.reshape(row_count, nirrep, -1, DMAX)
    valid_cols = jnp.arange(DMAX, dtype=jnp.int32)[None, :] < block_sizes[:, None]
    masked = jnp.where(valid_cols[None, :, None, :], blocked, jnp.zeros((), amplitudes.dtype))
    return masked.reshape(row_count, -1)


def general(amplitudes, integrals, block_sizes):
    masked = mask_slots(amplitudes, block_sizes)
    gathered = lax.all_gather(masked, "out", axis=0, tiled=True)
    own_columns = lax.all_to_all(gathered, "con", split_axis=1, concat_axis=0, tiled=True)
    out_count = lax.axis_size("out")
    con_count = lax.axis_size("con")
    per_device = masked.shape[0]
    own_columns = own_columns.reshape(con_count, out_count, per_device, -1)
    own_columns = jnp.transpose(own_columns, (1, 0, 2, 3)).reshape(
        con_count * out_count * per_device, -1
    )
    partial_sums = lax.dot_general(
        own_columns, integrals, (((1,), (1,)), ((), ())), preferred_element_type=jnp.float32
    )
    ladder = lax.psum_scatter(partial_sums, "con", scatter_dimension=0, tiled=True)
    return ladder.astype(jnp.bfloat16)


def roll(x, shift):
    return pltpu.roll(x.astype(jnp.float32), shift, 1).astype(x.dtype)


def pack_kernel(nirrep, cw, sizes_ref, amp_ref, out_ref):
    pairs = cw // 2
    rows = amp_ref.shape[0]
    lane = lax.broadcasted_iota(jnp.int32, (rows, LANES), 1)
    low = lane < LOW
    tiles = nirrep // 2
    extras = [[jnp.zeros((rows, LANES), amp_ref.dtype)] * tiles for _ in range(cw)]
    start = jnp.int32(0)
    for g in range(nirrep):
        extra = sizes_ref[g] - LOW
        inside = [
            (lane + k * LANES >= start) & (lane + k * LANES < start + extra) for k in range(tiles)
        ]
        shift = lax.rem(start, LANES)
        shift_half = lax.rem(start + LOW, LANES)
        for p in range(pairs):
            at = (g * pairs + p) * 3 * LANES
            one = amp_ref[:, at : at + LANES]
            two = amp_ref[:, at + LANES : at + 2 * LANES]
            three = amp_ref[:, at + 2 * LANES : at + 3 * LANES]
            to = (g * pairs + p) * LANES
            out_ref[:, to : to + LANES] = jnp.where(low, one, two)
            first = roll(jnp.where(low, two, one), shift_half)
            second = roll(three, shift)
            for k in range(tiles):
                extras[2 * p][k] = jnp.where(inside[k], first, extras[2 * p][k])
                extras[2 * p + 1][k] = jnp.where(inside[k], second, extras[2 * p + 1][k])
        start = start + extra
    base = nirrep * pairs * LANES
    for c in range(cw):
        for k in range(tiles):
            to = base + (c * tiles + k) * LANES
            out_ref[:, to : to + LANES] = extras[c][k]


def pack(amplitudes, block_sizes, cw):
    nirrep = block_sizes.shape[0]
    return pl.pallas_call(
        functools.partial(pack_kernel, nirrep, cw),
        out_shape=jax.ShapeDtypeStruct(
            (amplitudes.shape[0], nirrep * cw * LANES), amplitudes.dtype
        ),
        in_specs=[
            pl.BlockSpec(memory_space=pltpu.SMEM),
            pl.BlockSpec(memory_space=pltpu.VMEM),
        ],
        out_specs=pl.BlockSpec(memory_space=pltpu.VMEM),
        name="pack",
    )(block_sizes, amplitudes)


def unpack_rows(cw, nirrep, sizes_ref, con, piece, places, a_ref):
    pairs = cw // 2
    tiles = nirrep // 2
    base = nirrep * pairs * LANES
    rows = piece.shape[0]
    lane = lax.broadcasted_iota(jnp.int32, (rows, LANES), 1)
    low = lane < LOW
    own = nirrep // 2
    zero = jnp.zeros((rows, LANES), piece.dtype)
    start = jnp.int32(0)
    for g in range(own):
        start = start + jnp.where(con > 0, sizes_ref[g] - LOW, 0)
    for gg in range(own):
        g = con * own + gg
        extra = sizes_ref[g] - LOW
        tile = start // LANES
        shift = start - tile * LANES
        after = jnp.minimum(tile + 1, tiles - 1)
        tile = jnp.minimum(tile, tiles - 1)
        here = lane >= shift
        back = lax.rem(LANES - shift, LANES)
        back_half = lax.rem(LANES + LOW - shift, LANES)
        valid = lane < extra
        valid_half = jnp.where(low, lane + LOW, lane - LOW) < extra
        for p in range(pairs):
            at = pl.multiple_of((g * pairs + p) * LANES, LANES)
            both = piece[:, pl.ds(at, LANES)]
            halves = []
            for c in (2 * p, 2 * p + 1):
                one = piece[:, pl.ds(pl.multiple_of(base + (c * tiles + tile) * LANES, LANES), LANES)]
                two = piece[:, pl.ds(pl.multiple_of(base + (c * tiles + after) * LANES, LANES), LANES)]
                halves.append(jnp.where(here, one, two))
            first = jnp.where(valid_half, roll(halves[0], back_half), zero)
            second = jnp.where(valid, roll(halves[1], back), zero)
            to = (gg * pairs + p) * 3 * LANES
            values = (jnp.where(low, both, first), jnp.where(low, first, both), second)
            for i, place in enumerate(places):
                for t, value in enumerate(values):
                    a_ref[pl.ds(place, ROWS), to + t * LANES : to + (t + 1) * LANES] = value[
                        i * ROWS : (i + 1) * ROWS
                    ]
        start = start + extra


def contract_kernel(cw, nirrep, count, sizes_ref, con_ref, places_ref, *refs):
    pieces = refs[:count]
    w_ref, keep_ref, send_ref, a_ref = refs[count:]

    @pl.when(pl.program_id(0) == 0)
    def _():
        for n, piece in enumerate(pieces):
            places = [
                pl.multiple_of(places_ref[2 * n + i], ROWS) for i in range(piece.shape[0] // ROWS)
            ]
            unpack_rows(cw, nirrep, sizes_ref, con_ref[0], piece, places, a_ref)

    half = a_ref.shape[0] // 2
    sums = lax.dot_general(
        a_ref[...], w_ref[...], (((1,), (1,)), ((), ())), preferred_element_type=jnp.float32
    )
    keep_ref[...] = sums[:half]
    send_ref[...] = sums[half:]


def contract(sizes, con, places, pieces, integrals, cw):
    nirrep = sizes.shape[0]
    total = sum(p.shape[0] for p in pieces)
    n, k = integrals.shape
    block = 256
    half = jax.ShapeDtypeStruct((total // 2, n), jnp.float32)
    out_spec = pl.BlockSpec((total // 2, block), lambda i, *_: (0, i))
    return pl.pallas_call(
        functools.partial(contract_kernel, cw, nirrep, len(pieces)),
        out_shape=(half, half),
        grid_spec=pltpu.PrefetchScalarGridSpec(
            num_scalar_prefetch=3,
            grid=(n // block,),
            in_specs=[pl.BlockSpec(p.shape, lambda i, *_: (0, 0)) for p in pieces]
            + [pl.BlockSpec((block, k), lambda i, *_: (i, 0))],
            out_specs=(out_spec, out_spec),
            scratch_shapes=[pltpu.VMEM((total, k), jnp.bfloat16)],
        ),
        compiler_params=pltpu.CompilerParams(vmem_limit_bytes=48 * 2**20),
        name="contract",
    )(sizes, con.reshape(1), places, *pieces, integrals)


RING = (1, 3, 0, 2)
RING_BACK = (2, 0, 3, 1)


def chip_at(x, y, z):
    return (z * 2 + y) * 2 + x


def x_neighbour(o):
    return o ^ 1


def y_neighbour(o):
    return o ^ 2


def z_next(o):
    return RING[o // 4] * 4 + o % 4


def z_previous(o):
    return RING_BACK[o // 4] * 4 + o % 4


def ladder_of_16(amplitudes, integrals, block_sizes):
    out_count, con_count = lax.axis_size("out"), lax.axis_size("con")
    con = lax.axis_index("con")
    chip = lax.axis_index("out")

    def move(value, *by_core):
        pairs = [
            (o * con_count + c, by_core[c % len(by_core)](o) * con_count + c)
            for o in range(out_count)
            for c in range(con_count)
        ]
        return lax.ppermute(value, ("out", "con"), pairs)

    def swap_cores(value):
        return lax.ppermute(value, "con", [(0, 1), (1, 0)])

    cw = integrals.shape[1] // (block_sizes.shape[0] // con_count * DMAX)
    own = pack(amplitudes, block_sizes, cw)
    blocks = {0: own}
    blocks[1] = move(own, z_next)
    blocks[3] = move(own, z_previous)
    blocks[2] = move(blocks[1], z_next)
    pieces = []
    for k in (0, 1, 3, 2):
        there = move(blocks[k], x_neighbour, y_neighbour)
        both = jnp.concatenate([blocks[k], there])
        pieces += [both, move(both, y_neighbour, x_neighbour)]
    others = [swap_cores(piece) for piece in pieces]

    z = chip // 4
    inside = chip % 4
    ring_back = jnp.array(RING_BACK)
    planes = {0: z, 1: ring_back[z], 3: jnp.array(RING)[z], 2: 3 - z}
    places = []
    for core in (con, 1 - con):
        first = jnp.where(core == 0, inside ^ 1, inside ^ 2)
        second = jnp.where(core == 0, inside ^ 2, inside ^ 1)
        for k in (0, 1, 3, 2):
            for where in (inside, first, second, inside ^ 3):
                place = (planes[k] * 4 + where) * con_count + core
                places.append(place * ROWS)
    total = out_count * con_count * ROWS
    places = lax.rem(jnp.stack(places) + total - con * (total // 2), total)
    keep, send = contract(block_sizes, con, places, pieces + others, integrals, cw)
    return (keep + swap_cores(send)).astype(jnp.bfloat16)


def on_device(amplitudes, integrals, block_sizes):
    if amplitudes.shape[0] == ROWS and lax.axis_size("out") == 16:
        return ladder_of_16(amplitudes, integrals, block_sizes)
    return general(amplitudes, integrals, block_sizes)


def solution(mesh):
    in_specs = (P(("out", "con"), None), P("out", "con"), P())
    out_specs = P("con", "out")
    return jax.shard_map(
        on_device, mesh=mesh, in_specs=in_specs, out_specs=out_specs, check_vma=False
    )
```

```python
import functools

import jax
import jax.numpy as jnp
from jax import lax
from jax.experimental import pallas as pl
from jax.experimental.pallas import tpu as pltpu
from jax.sharding import PartitionSpec as P

DMAX = 192
LANES = 128
LOW = 64
ROWS = 16


def mask_slots(amplitudes, block_sizes):
    row_count = amplitudes.shape[0]
    nirrep = block_sizes.shape[0]
    blocked = amplitudes.reshape(row_count, nirrep, -1, DMAX)
    valid_cols = jnp.arange(DMAX, dtype=jnp.int32)[None, :] < block_sizes[:, None]
    masked = jnp.where(valid_cols[None, :, None, :], blocked, jnp.zeros((), amplitudes.dtype))
    return masked.reshape(row_count, -1)


def general(amplitudes, integrals, block_sizes):
    masked = mask_slots(amplitudes, block_sizes)
    gathered = lax.all_gather(masked, "out", axis=0, tiled=True)
    own_columns = lax.all_to_all(gathered, "con", split_axis=1, concat_axis=0, tiled=True)
    out_count = lax.axis_size("out")
    con_count = lax.axis_size("con")
    per_device = masked.shape[0]
    own_columns = own_columns.reshape(con_count, out_count, per_device, -1)
    own_columns = jnp.transpose(own_columns, (1, 0, 2, 3)).reshape(
        con_count * out_count * per_device, -1
    )
    partial_sums = lax.dot_general(
        own_columns, integrals, (((1,), (1,)), ((), ())), preferred_element_type=jnp.float32
    )
    ladder = lax.psum_scatter(partial_sums, "con", scatter_dimension=0, tiled=True)
    return ladder.astype(jnp.bfloat16)


def roll(x, shift):
    return pltpu.roll(x.astype(jnp.float32), shift, 1).astype(x.dtype)


def pack_kernel(nirrep, cw, sizes_ref, amp_ref, out_ref, both_ref):
    pairs = cw // 2
    rows = amp_ref.shape[0]
    lane = lax.broadcasted_iota(jnp.int32, (rows, LANES), 1)
    low = lane < LOW
    tiles = nirrep // 2
    extras = [[jnp.zeros((rows, LANES), amp_ref.dtype)] * tiles for _ in range(cw)]
    start = jnp.int32(0)
    for g in range(nirrep):
        extra = sizes_ref[g] - LOW
        inside = [
            (lane + k * LANES >= start) & (lane + k * LANES < start + extra) for k in range(tiles)
        ]
        shift = lax.rem(start, LANES)
        shift_half = lax.rem(start + LOW, LANES)
        for p in range(pairs):
            at = (g * pairs + p) * 3 * LANES
            one = amp_ref[:, at : at + LANES]
            two = amp_ref[:, at + LANES : at + 2 * LANES]
            three = amp_ref[:, at + 2 * LANES : at + 3 * LANES]
            to = (g * pairs + p) * LANES
            value = jnp.where(low, one, two)
            out_ref[:, to : to + LANES] = value
            both_ref[:rows, to : to + LANES] = value
            first = roll(jnp.where(low, two, one), shift_half)
            second = roll(three, shift)
            for k in range(tiles):
                extras[2 * p][k] = jnp.where(inside[k], first, extras[2 * p][k])
                extras[2 * p + 1][k] = jnp.where(inside[k], second, extras[2 * p + 1][k])
        start = start + extra
    base = nirrep * pairs * LANES
    for c in range(cw):
        for k in range(tiles):
            to = base + (c * tiles + k) * LANES
            out_ref[:, to : to + LANES] = extras[c][k]
            both_ref[:rows, to : to + LANES] = extras[c][k]


def pack(amplitudes, block_sizes, cw):
    nirrep = block_sizes.shape[0]
    rows, dtype = amplitudes.shape[0], amplitudes.dtype
    return pl.pallas_call(
        functools.partial(pack_kernel, nirrep, cw),
        out_shape=(
            jax.ShapeDtypeStruct((rows, nirrep * cw * LANES), dtype),
            jax.ShapeDtypeStruct((2 * rows, nirrep * cw * LANES), dtype),
        ),
        in_specs=[
            pl.BlockSpec(memory_space=pltpu.SMEM),
            pl.BlockSpec(memory_space=pltpu.VMEM),
        ],
        out_specs=(
            pl.BlockSpec(memory_space=pltpu.VMEM),
            pl.BlockSpec(memory_space=pltpu.VMEM),
        ),
        name="pack",
    )(block_sizes, amplitudes)


def unpack_rows(cw, nirrep, sizes_ref, con, packed, places, a_ref):
    pairs = cw // 2
    tiles = nirrep // 2
    own = nirrep // 2
    base = own * pairs * LANES
    rows = packed.shape[0]
    lane = lax.broadcasted_iota(jnp.int32, (rows, LANES), 1)
    low = lane < LOW
    zero = jnp.zeros((rows, LANES), packed.dtype)

    def one_irrep(g, start):
        extra = sizes_ref[con * own + g] - LOW
        tile = start // LANES
        shift = start - tile * LANES
        after = jnp.minimum(tile + 1, tiles - 1)
        tile = jnp.minimum(tile, tiles - 1)
        here = lane >= shift
        back = lax.rem(LANES - shift, LANES)
        back_half = lax.rem(LANES + LOW - shift, LANES)
        valid = lane < extra
        valid_half = jnp.where(low, lane + LOW, lane - LOW) < extra
        for p in range(pairs):
            at = pl.multiple_of((g * pairs + p) * LANES, LANES)
            both = packed[:, pl.ds(at, LANES)]
            halves = []
            for c in (2 * p, 2 * p + 1):
                one = packed[:, pl.ds(pl.multiple_of(base + (c * tiles + tile) * LANES, LANES), LANES)]
                two = packed[:, pl.ds(pl.multiple_of(base + (c * tiles + after) * LANES, LANES), LANES)]
                halves.append(jnp.where(here, one, two))
            first = jnp.where(valid_half, roll(halves[0], back_half), zero)
            second = jnp.where(valid, roll(halves[1], back), zero)
            to = pl.multiple_of((g * pairs + p) * 3 * LANES, LANES)
            values = (jnp.where(low, both, first), jnp.where(low, first, both), second)
            for i, place in enumerate(places):
                for t, value in enumerate(values):
                    a_ref[pl.ds(place, ROWS), pl.ds(to + t * LANES, LANES)] = value[
                        i * ROWS : (i + 1) * ROWS
                    ]
        return start + extra

    start = jnp.int32(0)
    for g in range(own):
        start = start + jnp.where(con > 0, sizes_ref[g] - LOW, 0)
    lax.fori_loop(0, own, one_irrep, start)


PLANE = 4 * 2 * ROWS
SMEM = pl.BlockSpec(memory_space=pltpu.SMEM)
VMEM = pl.BlockSpec(memory_space=pltpu.VMEM)
HBM = pl.BlockSpec(memory_space=pltpu.HBM)
ANY = pl.BlockSpec(memory_space=pl.ANY)


def contract_kernel(cw, nirrep, count, numbers_ref, *refs):
    sizes_ref = numbers_ref
    chip, con = numbers_ref[nirrep], numbers_ref[nirrep + 1]
    z, inside = chip // 4, chip % 4
    pieces = refs[:count]
    w_hbm, keep_ref, send_out, a_ref, w_ref, pieces_ref, send_ref, sems, w_sems, out_sems = refs[count:]
    block = w_ref.shape[0] // w_sems.shape[0]
    half = send_ref.shape[0]
    total = 2 * half
    depth = pieces[0].shape[0]
    per_plane = PLANE // depth
    width = w_ref.shape[1] // 3
    copies = []
    for n, piece in enumerate(pieces):
        rows = pl.ds(n % per_plane * depth, depth)
        to = pieces_ref.at[n // per_plane]
        copies += [
            pltpu.make_async_copy(
                piece.at[:, pl.ds(pl.multiple_of(con * width, LANES), width)],
                to.at[rows, pl.ds(0, width)],
                sems.at[n, 0],
            ),
            pltpu.make_async_copy(
                piece.at[:, pl.ds(2 * width, 2 * width)],
                to.at[rows, pl.ds(width, 2 * width)],
                sems.at[n, 1],
            ),
        ]
    w_copies = [
        pltpu.make_async_copy(
            w_hbm.at[pl.ds(n * block, block)], w_ref.at[pl.ds(n * block, block)], w_sems.at[n]
        )
        for n in range(w_sems.shape[0])
    ]
    for copy in copies + w_copies:
        copy.start()
    plane_before = jnp.where(z == 0, 2, jnp.where(z == 1, 0, jnp.where(z == 2, 3, 1)))
    planes = (z, plane_before, 3 - plane_before, 3 - z)

    @pl.loop(0, count // per_plane)
    def _(k):
        plane = jnp.where(
            k == 0, planes[0], jnp.where(k == 1, planes[1], jnp.where(k == 2, planes[2], planes[3]))
        )
        places = []
        for n in range(per_plane):
            core = con if n < 2 else 1 - con
            chips = (inside, inside ^ (1 + core)) if n % 2 == 0 else (inside ^ (2 - core), inside ^ 3)
            for c in chips:
                place = ((plane * 4 + c) * 2 + core) * ROWS + total - con * half
                places.append(pl.multiple_of(lax.rem(place, total), ROWS))
            rows = pieces_ref.at[k, pl.ds(n * depth, depth)]
            for i, part in enumerate((pl.ds(0, width), pl.ds(width, 2 * width))):
                at = rows.at[:, part]
                pltpu.make_async_copy(at, at, sems.at[k * per_plane + n, i]).wait()
        unpack_rows(cw, nirrep, sizes_ref, con, pieces_ref.at[k], places, a_ref)

    def send_copy(n):
        columns = pl.ds(pl.multiple_of(n * block, block), block)
        return pltpu.make_async_copy(
            send_ref.at[:, columns], send_out.at[:, columns], out_sems.at[n]
        )

    @pl.loop(0, w_sems.shape[0])
    def _(n):
        columns = pl.ds(pl.multiple_of(n * block, block), block)
        pltpu.make_async_copy(w_ref.at[columns], w_ref.at[columns], w_sems.at[n]).wait()
        sums = lax.dot_general(
            a_ref[...],
            w_ref[columns, :],
            (((1,), (1,)), ((), ())),
            preferred_element_type=jnp.float32,
        )
        keep_ref[:, columns] = sums[:half]
        send_ref[:, columns] = sums[half:]
        send_copy(n).start()

    @pl.loop(0, w_sems.shape[0])
    def _(n):
        send_copy(n).wait()


def contract(numbers, pieces, integrals, cw, nirrep):
    n, k = integrals.shape
    count = len(pieces)
    total = sum(piece.shape[0] for piece in pieces)
    half = jax.ShapeDtypeStruct((total // 2, n), jnp.float32)
    return pl.pallas_call(
        functools.partial(contract_kernel, cw, nirrep, count),
        out_shape=(pltpu.VMEM(half.shape, half.dtype), half),
        in_specs=[SMEM] + [ANY] * count + [HBM],
        out_specs=(VMEM, HBM),
        scratch_shapes=[
            pltpu.VMEM((total, k), jnp.bfloat16),
            pltpu.VMEM((n, k), jnp.bfloat16),
            pltpu.VMEM((total // PLANE, PLANE, k), jnp.bfloat16),
            pltpu.VMEM((total // 2, n), jnp.float32),
            pltpu.SemaphoreType.DMA((count, 2)),
            pltpu.SemaphoreType.DMA((n // 256,)),
            pltpu.SemaphoreType.DMA((n // 256,)),
        ],
        compiler_params=pltpu.CompilerParams(vmem_limit_bytes=44 * 2**20),
        name="contract",
    )(numbers, *pieces, integrals)


def add_kernel(keep_ref, got_ref, out, out_ref, sems):
    parts = sems.shape[0]
    rows = out_ref.shape[0] // parts

    def copy_out(n):
        part = pl.ds(pl.multiple_of(n * rows, rows), rows)
        return pltpu.make_async_copy(out_ref.at[part], out.at[part], sems.at[n])

    @pl.loop(0, parts)
    def _(n):
        part = pl.ds(pl.multiple_of(n * rows, rows), rows)
        out_ref[part] = (keep_ref[part] + got_ref[part]).astype(out_ref.dtype)
        copy_out(n).start()

    @pl.loop(0, parts)
    def _(n):
        copy_out(n).wait()


def add(keep, got):
    keep, got = (pltpu.with_memory_space_constraint(x, pltpu.VMEM) for x in (keep, got))
    return pl.pallas_call(
        add_kernel,
        out_shape=jax.ShapeDtypeStruct(keep.shape, jnp.bfloat16),
        in_specs=[VMEM, VMEM],
        out_specs=HBM,
        scratch_shapes=[pltpu.VMEM(keep.shape, jnp.bfloat16), pltpu.SemaphoreType.DMA((4,))],
        compiler_params=pltpu.CompilerParams(vmem_limit_bytes=4 * 2**20),
        name="add",
    )(keep, got)


RING = (1, 3, 0, 2)
RING_BACK = (2, 0, 3, 1)


def x_neighbour(o):
    return o ^ 1


def y_neighbour(o):
    return o ^ 2


def z_next(o):
    return RING[o // 4] * 4 + o % 4


def z_previous(o):
    return RING_BACK[o // 4] * 4 + o % 4


def after(value, *others):
    return lax.optimization_barrier((value, *others))[0]


STEPS = {
    "z1": (("own",), "next"),
    "f0": (("own",), "first"),
    "z3": (("own",), "previous"),
    "s0": (("own", "f0"), "second"),
    "z2": (("z1",), "next"),
    "f1": (("z1",), "first"),
    "f3": (("z3",), "first"),
    "s1": (("s0",), "next"),
    "f2": (("z2",), "first"),
    "s3": (("z3", "f3"), "second"),
    "s2": (("z2", "f2"), "second"),
}
AFTER = {"z3": ("f0",), "f3": ("s0",), "f2": ("f1",)}


def ladder_of_16(amplitudes, integrals, block_sizes):
    out_count, con_count = lax.axis_size("out"), lax.axis_size("con")
    ways = {
        "next": (z_next,),
        "previous": (z_previous,),
        "first": (x_neighbour, y_neighbour),
        "second": (y_neighbour, x_neighbour),
    }

    def move(value, way):
        by_core = ways[way]
        pairs = [
            (o * con_count + c, by_core[c % len(by_core)](o) * con_count + c)
            for o in range(out_count)
            for c in range(con_count)
        ]
        return lax.ppermute(value, ("out", "con"), pairs)

    def swap_cores(value):
        return lax.ppermute(value, "con", [(0, 1), (1, 0)])

    cw = integrals.shape[1] // (block_sizes.shape[0] // con_count * DMAX)
    here = jnp.stack([lax.axis_index("out"), lax.axis_index("con")]).astype(jnp.int32)
    numbers = jnp.concatenate([block_sizes, here])
    own, own_top = pack(amplitudes, block_sizes, cw)
    arrays = {("own",): own}

    def get(names):
        if names not in arrays:
            one, two = (arrays[(name,)] for name in names)
            if names[0] == "own":
                arrays[names] = lax.dynamic_update_slice(own_top, two, (ROWS, 0))
            else:
                arrays[names] = jnp.concatenate([one, two])
        return arrays[names]

    steps = dict(STEPS)
    while steps:
        name = next(
            n
            for n, (sent, _) in steps.items()
            if all((o,) in arrays for o in sent + AFTER.get(n, ()))
        )
        sent, way = steps.pop(name)
        others = [arrays[(o,)] for o in AFTER.get(name, ())]
        if name == "z2":
            others.append(numbers)
        value = get(sent)
        arrays[(name,)] = move(after(value, *others) if others else value, way)

    pieces = []
    for k, z in enumerate(("own", "z1", "z3", "z2")):
        f, s = f"f{z[1:]}" if k else "f0", f"s{z[1:]}" if k else "s0"
        plane = [get((z, f)), arrays[(s,)]]
        pieces += plane + [swap_cores(piece) for piece in plane]
    keep, send = contract(numbers, pieces, integrals, cw, block_sizes.shape[0])
    return add(keep, swap_cores(send))


def on_device(amplitudes, integrals, block_sizes):
    if amplitudes.shape[0] == ROWS and lax.axis_size("out") == 16:
        return ladder_of_16(amplitudes, integrals, block_sizes)
    return general(amplitudes, integrals, block_sizes)


def solution(mesh):
    in_specs = (P(("out", "con"), None), P("out", "con"), P())
    out_specs = P("con", "out")
    return jax.shard_map(
        on_device, mesh=mesh, in_specs=in_specs, out_specs=out_specs, check_vma=False
    )
```

```python
import functools

import jax
import jax.numpy as jnp
from jax import lax
from jax.experimental import pallas as pl
from jax.experimental.pallas import tpu as pltpu
from jax.sharding import PartitionSpec as P

DMAX = 192
LANES = 128
LOW = 64
ROWS = 16


def mask_slots(amplitudes, block_sizes):
    row_count = amplitudes.shape[0]
    nirrep = block_sizes.shape[0]
    blocked = amplitudes.reshape(row_count, nirrep, -1, DMAX)
    valid_cols = jnp.arange(DMAX, dtype=jnp.int32)[None, :] < block_sizes[:, None]
    masked = jnp.where(valid_cols[None, :, None, :], blocked, jnp.zeros((), amplitudes.dtype))
    return masked.reshape(row_count, -1)


def general(amplitudes, integrals, block_sizes):
    masked = mask_slots(amplitudes, block_sizes)
    gathered = lax.all_gather(masked, "out", axis=0, tiled=True)
    own_columns = lax.all_to_all(gathered, "con", split_axis=1, concat_axis=0, tiled=True)
    out_count = lax.axis_size("out")
    con_count = lax.axis_size("con")
    per_device = masked.shape[0]
    own_columns = own_columns.reshape(con_count, out_count, per_device, -1)
    own_columns = jnp.transpose(own_columns, (1, 0, 2, 3)).reshape(
        con_count * out_count * per_device, -1
    )
    partial_sums = lax.dot_general(
        own_columns, integrals, (((1,), (1,)), ((), ())), preferred_element_type=jnp.float32
    )
    ladder = lax.psum_scatter(partial_sums, "con", scatter_dimension=0, tiled=True)
    return ladder.astype(jnp.bfloat16)


def roll(x, shift):
    return pltpu.roll(x.astype(jnp.float32), shift, 1).astype(x.dtype)


def pack_kernel(nirrep, cw, sizes_ref, amp_ref, out_ref, both_ref):
    pairs = cw // 2
    rows = amp_ref.shape[0]
    lane = lax.broadcasted_iota(jnp.int32, (rows, LANES), 1)
    low = lane < LOW
    tiles = nirrep // 2
    extras = [[jnp.zeros((rows, LANES), amp_ref.dtype)] * tiles for _ in range(cw)]
    start = jnp.int32(0)
    for g in range(nirrep):
        extra = sizes_ref[g] - LOW
        inside = [
            (lane + k * LANES >= start) & (lane + k * LANES < start + extra) for k in range(tiles)
        ]
        shift = lax.rem(start, LANES)
        shift_half = lax.rem(start + LOW, LANES)
        for p in range(pairs):
            at = (g * pairs + p) * 3 * LANES
            one = amp_ref[:, at : at + LANES]
            two = amp_ref[:, at + LANES : at + 2 * LANES]
            three = amp_ref[:, at + 2 * LANES : at + 3 * LANES]
            to = (g * pairs + p) * LANES
            value = jnp.where(low, one, two)
            out_ref[:, to : to + LANES] = value
            both_ref[:rows, to : to + LANES] = value
            first = roll(jnp.where(low, two, one), shift_half)
            second = roll(three, shift)
            for k in range(tiles):
                extras[2 * p][k] = jnp.where(inside[k], first, extras[2 * p][k])
                extras[2 * p + 1][k] = jnp.where(inside[k], second, extras[2 * p + 1][k])
        start = start + extra
    base = nirrep * pairs * LANES
    for c in range(cw):
        for k in range(tiles):
            to = base + (c * tiles + k) * LANES
            out_ref[:, to : to + LANES] = extras[c][k]
            both_ref[:rows, to : to + LANES] = extras[c][k]


def pack(amplitudes, block_sizes, cw):
    nirrep = block_sizes.shape[0]
    rows, dtype = amplitudes.shape[0], amplitudes.dtype
    return pl.pallas_call(
        functools.partial(pack_kernel, nirrep, cw),
        out_shape=(
            jax.ShapeDtypeStruct((rows, nirrep * cw * LANES), dtype),
            jax.ShapeDtypeStruct((2 * rows, nirrep * cw * LANES), dtype),
        ),
        in_specs=[
            pl.BlockSpec(memory_space=pltpu.SMEM),
            pl.BlockSpec(memory_space=pltpu.VMEM),
        ],
        out_specs=(
            pl.BlockSpec(memory_space=pltpu.VMEM),
            pl.BlockSpec(memory_space=pltpu.VMEM),
        ),
        name="pack",
    )(block_sizes, amplitudes)


def unpack_rows(cw, nirrep, sizes_ref, con, packed, places, a_ref):
    pairs = cw // 2
    tiles = nirrep // 2
    own = nirrep // 2
    base = own * pairs * LANES
    rows = packed.shape[0]
    lane = lax.broadcasted_iota(jnp.int32, (rows, LANES), 1)
    low = lane < LOW
    zero = jnp.zeros((rows, LANES), packed.dtype)

    def one_irrep(g, start):
        extra = sizes_ref[con * own + g] - LOW
        tile = start // LANES
        shift = start - tile * LANES
        after = jnp.minimum(tile + 1, tiles - 1)
        tile = jnp.minimum(tile, tiles - 1)
        here = lane >= shift
        back = lax.rem(LANES - shift, LANES)
        back_half = lax.rem(LANES + LOW - shift, LANES)
        valid = lane < extra
        valid_half = jnp.where(low, lane + LOW, lane - LOW) < extra
        for p in range(pairs):
            at = pl.multiple_of((g * pairs + p) * LANES, LANES)
            both = packed[:, pl.ds(at, LANES)]
            halves = []
            for c in (2 * p, 2 * p + 1):
                one = packed[:, pl.ds(pl.multiple_of(base + (c * tiles + tile) * LANES, LANES), LANES)]
                two = packed[:, pl.ds(pl.multiple_of(base + (c * tiles + after) * LANES, LANES), LANES)]
                halves.append(jnp.where(here, one, two))
            first = jnp.where(valid_half, roll(halves[0], back_half), zero)
            second = jnp.where(valid, roll(halves[1], back), zero)
            to = pl.multiple_of((g * pairs + p) * 3 * LANES, LANES)
            values = (jnp.where(low, both, first), jnp.where(low, first, both), second)
            for i, place in enumerate(places):
                for t, value in enumerate(values):
                    a_ref[pl.ds(place, ROWS), pl.ds(to + t * LANES, LANES)] = value[
                        i * ROWS : (i + 1) * ROWS
                    ]
        return start + extra

    start = jnp.int32(0)
    for g in range(own):
        start = start + jnp.where(con > 0, sizes_ref[g] - LOW, 0)
    lax.fori_loop(0, own, one_irrep, start)


PLANE = 4 * 2 * ROWS
SMEM = pl.BlockSpec(memory_space=pltpu.SMEM)
VMEM = pl.BlockSpec(memory_space=pltpu.VMEM)
HBM = pl.BlockSpec(memory_space=pltpu.HBM)
ANY = pl.BlockSpec(memory_space=pl.ANY)


def fetch(con, width, pieces, packed_ref, sems):
    depth = pieces[0].shape[0]
    copies = []
    for n, piece in enumerate(pieces):
        rows = pl.ds(n * depth, depth)
        copies += [
            pltpu.make_async_copy(
                piece.at[:, pl.ds(pl.multiple_of(con * width, LANES), width)],
                packed_ref.at[rows, pl.ds(0, width)],
                sems.at[n, 0],
            ),
            pltpu.make_async_copy(
                piece.at[:, pl.ds(2 * width, 2 * width)],
                packed_ref.at[rows, pl.ds(width, 2 * width)],
                sems.at[n, 1],
            ),
        ]
    return copies


def places_in_plane(chip, con):
    inside = chip % 4
    places = []
    for core in (con, 1 - con):
        for c in (inside, inside ^ (1 + core), inside ^ (2 - core), inside ^ 3):
            places.append((c * 2 + core) * ROWS)
    return places


def unpack_kernel(cw, nirrep, numbers_ref, *refs):
    pieces = refs[:4]
    out, a_ref, packed_ref, sems, out_sem = refs[4:]
    chip, con = numbers_ref[nirrep], numbers_ref[nirrep + 1]
    copies = fetch(con, a_ref.shape[1] // 3, pieces, packed_ref, sems)
    for copy in copies:
        copy.start()
    for copy in copies:
        copy.wait()
    places = [pl.multiple_of(place, ROWS) for place in places_in_plane(chip, con)]
    unpack_rows(cw, nirrep, numbers_ref, con, packed_ref, places, a_ref)
    copy = pltpu.make_async_copy(a_ref, out, out_sem)
    copy.start()
    copy.wait()


def unpack(numbers, pieces, cw, nirrep, flops):
    k = nirrep // 2 * cw * DMAX
    return pl.pallas_call(
        functools.partial(unpack_kernel, cw, nirrep),
        out_shape=jax.ShapeDtypeStruct((PLANE, k), jnp.bfloat16),
        in_specs=[SMEM] + [ANY] * 4,
        out_specs=HBM,
        scratch_shapes=[
            pltpu.VMEM((PLANE, k), jnp.bfloat16),
            pltpu.VMEM((PLANE, k), jnp.bfloat16),
            pltpu.SemaphoreType.DMA((4, 2)),
            pltpu.SemaphoreType.DMA,
        ],
        compiler_params=pltpu.CompilerParams(vmem_limit_bytes=44 * 2**20),
        cost_estimate=pl.CostEstimate(flops=flops, bytes_accessed=4 * PLANE * k, transcendentals=0),
        name="unpack",
    )(numbers, *pieces)


def contract_kernel(cw, nirrep, ready, packed, numbers_ref, *refs):
    chip, con = numbers_ref[nirrep], numbers_ref[nirrep + 1]
    z = chip // 4
    rows_ready, pieces = refs[: len(ready)], refs[len(ready) : len(ready) + 4 * len(packed)]
    refs = refs[len(ready) + 4 * len(packed) :]
    w_hbm, keep_ref, send_out, a_ref, w_ref, packed_ref, send_ref, sems, r_sems, w_sems, out_sems = refs
    block = w_ref.shape[0] // w_sems.shape[0]
    half = send_ref.shape[0]
    total = 2 * half
    width = w_ref.shape[1] // 3
    before = jnp.where(z == 0, 2, jnp.where(z == 1, 0, jnp.where(z == 2, 3, 1)))
    planes = {0: z, 1: before, 3: 3 - before, 2: 3 - z}

    def start_of(plane):
        return pl.multiple_of(lax.rem(plane * PLANE + total - con * half, total), PLANE)

    copies = []
    for n in range(len(packed)):
        copies += fetch(con, width, pieces[4 * n : 4 * n + 4], packed_ref.at[n], sems.at[n])
    r_copies = [
        pltpu.make_async_copy(rows, a_ref.at[pl.ds(start_of(planes[k]), PLANE)], r_sems.at[n])
        for n, (k, rows) in enumerate(zip(ready, rows_ready))
    ]
    w_copies = [
        pltpu.make_async_copy(
            w_hbm.at[pl.ds(n * block, block)], w_ref.at[pl.ds(n * block, block)], w_sems.at[n]
        )
        for n in range(w_sems.shape[0])
    ]
    for copy in copies + w_copies[:1] + r_copies + w_copies[1:]:
        copy.start()
    inner = places_in_plane(chip, con)

    @pl.loop(0, len(packed))
    def _(n):
        plane = planes[packed[0]]
        for i, k in enumerate(packed[1:]):
            plane = jnp.where(n == i + 1, planes[k], plane)
        places = [pl.multiple_of(start_of(plane) + place, ROWS) for place in inner]
        for copy in fetch(con, width, pieces[:4], packed_ref.at[n], sems.at[n]):
            copy.wait()
        unpack_rows(cw, nirrep, numbers_ref, con, packed_ref.at[n], places, a_ref)

    for copy in r_copies:
        copy.wait()

    def send_copy(n):
        columns = pl.ds(pl.multiple_of(n * block, block), block)
        return pltpu.make_async_copy(
            send_ref.at[:, columns], send_out.at[:, columns], out_sems.at[n]
        )

    @pl.loop(0, w_sems.shape[0])
    def _(n):
        columns = pl.ds(pl.multiple_of(n * block, block), block)
        pltpu.make_async_copy(w_ref.at[columns], w_ref.at[columns], w_sems.at[n]).wait()
        sums = lax.dot_general(
            a_ref[...],
            w_ref[columns, :],
            (((1,), (1,)), ((), ())),
            preferred_element_type=jnp.float32,
        )
        keep_ref[:, columns] = sums[:half]
        send_ref[:, columns] = sums[half:]
        send_copy(n).start()

    @pl.loop(0, w_sems.shape[0])
    def _(n):
        send_copy(n).wait()


def contract(numbers, ready, packed, integrals, cw, nirrep):
    n, k = integrals.shape
    total = PLANE * (len(ready) + len(packed))
    half = jax.ShapeDtypeStruct((total // 2, n), jnp.float32)
    pieces = [piece for plane in packed.values() for piece in plane]
    return pl.pallas_call(
        functools.partial(contract_kernel, cw, nirrep, tuple(ready), tuple(packed)),
        out_shape=(pltpu.VMEM(half.shape, half.dtype), half),
        in_specs=[SMEM] + [HBM] * len(ready) + [ANY] * len(pieces) + [HBM],
        out_specs=(VMEM, HBM),
        scratch_shapes=[
            pltpu.VMEM((total, k), jnp.bfloat16),
            pltpu.VMEM((n, k), jnp.bfloat16),
            pltpu.VMEM((len(packed), PLANE, k), jnp.bfloat16),
            pltpu.VMEM((total // 2, n), jnp.float32),
            pltpu.SemaphoreType.DMA((len(packed), 4, 2)),
            pltpu.SemaphoreType.DMA((len(ready) + 1,)),
            pltpu.SemaphoreType.DMA((n // 256,)),
            pltpu.SemaphoreType.DMA((n // 256,)),
        ],
        compiler_params=pltpu.CompilerParams(vmem_limit_bytes=44 * 2**20),
        name="contract",
    )(numbers, *ready.values(), *pieces, integrals)


def add_kernel(keep_ref, got_ref, out, out_ref, sems):
    parts = sems.shape[0]
    rows = out_ref.shape[0] // parts

    def copy_out(n):
        part = pl.ds(pl.multiple_of(n * rows, rows), rows)
        return pltpu.make_async_copy(out_ref.at[part], out.at[part], sems.at[n])

    @pl.loop(0, parts)
    def _(n):
        part = pl.ds(pl.multiple_of(n * rows, rows), rows)
        out_ref[part] = (keep_ref[part] + got_ref[part]).astype(out_ref.dtype)
        copy_out(n).start()

    @pl.loop(0, parts)
    def _(n):
        copy_out(n).wait()


def add(keep, got):
    keep, got = (pltpu.with_memory_space_constraint(x, pltpu.VMEM) for x in (keep, got))
    return pl.pallas_call(
        add_kernel,
        out_shape=jax.ShapeDtypeStruct(keep.shape, jnp.bfloat16),
        in_specs=[VMEM, VMEM],
        out_specs=HBM,
        scratch_shapes=[pltpu.VMEM(keep.shape, jnp.bfloat16), pltpu.SemaphoreType.DMA((4,))],
        compiler_params=pltpu.CompilerParams(vmem_limit_bytes=4 * 2**20),
        name="add",
    )(keep, got)


RING = (1, 3, 0, 2)
RING_BACK = (2, 0, 3, 1)


def x_neighbour(o):
    return o ^ 1


def y_neighbour(o):
    return o ^ 2


def z_next(o):
    return RING[o // 4] * 4 + o % 4


def z_previous(o):
    return RING_BACK[o // 4] * 4 + o % 4


def after(value, *others):
    return lax.optimization_barrier((value, *others))[0]


STEPS = {
    "z1": (("own",), "next"),
    "f0": (("own",), "first"),
    "z3": (("own",), "previous"),
    "s0": (("own", "f0"), "second"),
    "z2": (("z1",), "next"),
    "f1": (("z1",), "first"),
    "f3": (("z3",), "first"),
    "s1": (("s0",), "next"),
    "f2": (("z2",), "first"),
    "s3": (("z3", "f3"), "second"),
    "s2": (("z2", "f2"), "second"),
}
AFTER = {"z3": ("f0",), "f3": ("s0",), "f2": ("f1",)}
READY = {0: 10**10}


def ladder_of_16(amplitudes, integrals, block_sizes):
    out_count, con_count = lax.axis_size("out"), lax.axis_size("con")
    ways = {
        "next": (z_next,),
        "previous": (z_previous,),
        "first": (x_neighbour, y_neighbour),
        "second": (y_neighbour, x_neighbour),
    }

    def move(value, way):
        by_core = ways[way]
        pairs = [
            (o * con_count + c, by_core[c % len(by_core)](o) * con_count + c)
            for o in range(out_count)
            for c in range(con_count)
        ]
        return lax.ppermute(value, ("out", "con"), pairs)

    def swap_cores(value):
        return lax.ppermute(value, "con", [(0, 1), (1, 0)])

    cw = integrals.shape[1] // (block_sizes.shape[0] // con_count * DMAX)
    here = jnp.stack([lax.axis_index("out"), lax.axis_index("con")]).astype(jnp.int32)
    numbers = jnp.concatenate([block_sizes, here])
    own, own_top = pack(amplitudes, block_sizes, cw)
    arrays = {("own",): own}

    def get(names):
        if names not in arrays:
            one, two = (arrays[(name,)] for name in names)
            if names[0] == "own":
                arrays[names] = lax.dynamic_update_slice(own_top, two, (ROWS, 0))
            else:
                arrays[names] = jnp.concatenate([one, two])
        return arrays[names]

    steps = dict(STEPS)
    while steps:
        name = next(
            n
            for n, (sent, _) in steps.items()
            if all((o,) in arrays for o in sent + AFTER.get(n, ()))
        )
        sent, way = steps.pop(name)
        others = [arrays[(o,)] for o in AFTER.get(name, ())]
        if name == "z2":
            others.append(numbers)
        value = get(sent)
        arrays[(name,)] = move(after(value, *others) if others else value, way)

    nirrep = block_sizes.shape[0]
    ready, packed = {}, {}
    for k, z in ((0, "own"), (1, "z1"), (3, "z3"), (2, "z2")):
        plane = [get((z, f"f{k}")), arrays[(f"s{k}",)]]
        plane += [swap_cores(piece) for piece in plane]
        if k in READY:
            ready[k] = unpack(numbers, plane, cw, nirrep, READY[k])
        else:
            packed[k] = plane
    keep, send = contract(numbers, ready, packed, integrals, cw, nirrep)
    return add(keep, swap_cores(send))


def on_device(amplitudes, integrals, block_sizes):
    if amplitudes.shape[0] == ROWS and lax.axis_size("out") == 16:
        return ladder_of_16(amplitudes, integrals, block_sizes)
    return general(amplitudes, integrals, block_sizes)


def solution(mesh):
    in_specs = (P(("out", "con"), None), P("out", "con"), P())
    out_specs = P("con", "out")
    return jax.shard_map(
        on_device, mesh=mesh, in_specs=in_specs, out_specs=out_specs, check_vma=False
    )
```

```python
import functools

import jax
import jax.numpy as jnp
from jax import lax
from jax.experimental import pallas as pl
from jax.experimental.pallas import tpu as pltpu
from jax.sharding import PartitionSpec as P

DMAX = 192
LANES = 128
LOW = 64
ROWS = 16


def mask_slots(amplitudes, block_sizes):
    row_count = amplitudes.shape[0]
    nirrep = block_sizes.shape[0]
    blocked = amplitudes.reshape(row_count, nirrep, -1, DMAX)
    valid_cols = jnp.arange(DMAX, dtype=jnp.int32)[None, :] < block_sizes[:, None]
    masked = jnp.where(valid_cols[None, :, None, :], blocked, jnp.zeros((), amplitudes.dtype))
    return masked.reshape(row_count, -1)


def general(amplitudes, integrals, block_sizes):
    masked = mask_slots(amplitudes, block_sizes)
    gathered = lax.all_gather(masked, "out", axis=0, tiled=True)
    own_columns = lax.all_to_all(gathered, "con", split_axis=1, concat_axis=0, tiled=True)
    out_count = lax.axis_size("out")
    con_count = lax.axis_size("con")
    per_device = masked.shape[0]
    own_columns = own_columns.reshape(con_count, out_count, per_device, -1)
    own_columns = jnp.transpose(own_columns, (1, 0, 2, 3)).reshape(
        con_count * out_count * per_device, -1
    )
    partial_sums = lax.dot_general(
        own_columns, integrals, (((1,), (1,)), ((), ())), preferred_element_type=jnp.float32
    )
    ladder = lax.psum_scatter(partial_sums, "con", scatter_dimension=0, tiled=True)
    return ladder.astype(jnp.bfloat16)


def roll(x, shift):
    return pltpu.roll(x, shift, 1)


def pack_kernel(nirrep, cw, sizes_ref, amp_ref, out_ref, both_ref):
    pairs = cw // 2
    rows = amp_ref.shape[0]
    lane = lax.broadcasted_iota(jnp.int32, (rows, LANES), 1)
    low = lane < LOW
    tiles = nirrep // 2
    extras = [[jnp.zeros((rows, LANES), amp_ref.dtype)] * tiles for _ in range(cw)]
    start = jnp.int32(0)
    for g in range(nirrep):
        extra = sizes_ref[g] - LOW
        inside = [
            (lane + k * LANES >= start) & (lane + k * LANES < start + extra) for k in range(tiles)
        ]
        shift = lax.rem(start, LANES)
        shift_half = lax.rem(start + LOW, LANES)
        for p in range(pairs):
            at = (g * pairs + p) * 3 * LANES
            one = amp_ref[:, at : at + LANES]
            two = amp_ref[:, at + LANES : at + 2 * LANES]
            three = amp_ref[:, at + 2 * LANES : at + 3 * LANES]
            to = (g * pairs + p) * LANES
            value = jnp.where(low, one, two)
            out_ref[:, to : to + LANES] = value
            both_ref[:rows, to : to + LANES] = value
            first = roll(jnp.where(low, two, one), shift_half)
            second = roll(three, shift)
            for k in range(tiles):
                extras[2 * p][k] = jnp.where(inside[k], first, extras[2 * p][k])
                extras[2 * p + 1][k] = jnp.where(inside[k], second, extras[2 * p + 1][k])
        start = start + extra
    base = nirrep * pairs * LANES
    for c in range(cw):
        for k in range(tiles):
            to = base + (c * tiles + k) * LANES
            out_ref[:, to : to + LANES] = extras[c][k]
            both_ref[:rows, to : to + LANES] = extras[c][k]


def pack(amplitudes, block_sizes, cw):
    nirrep = block_sizes.shape[0]
    rows, dtype = amplitudes.shape[0], amplitudes.dtype
    return pl.pallas_call(
        functools.partial(pack_kernel, nirrep, cw),
        out_shape=(
            jax.ShapeDtypeStruct((rows, nirrep * cw * LANES), dtype),
            jax.ShapeDtypeStruct((2 * rows, nirrep * cw * LANES), dtype),
        ),
        in_specs=[
            pl.BlockSpec(memory_space=pltpu.SMEM),
            pl.BlockSpec(memory_space=pltpu.VMEM),
        ],
        out_specs=(
            pl.BlockSpec(memory_space=pltpu.VMEM),
            pl.BlockSpec(memory_space=pltpu.VMEM),
        ),
        name="pack",
    )(block_sizes, amplitudes)


def unpack_rows(cw, nirrep, sizes_ref, con, packed, places, a_ref):
    pairs = cw // 2
    tiles = nirrep // 2
    own = nirrep // 2
    base = own * pairs * LANES
    rows = packed.shape[0]
    lane = lax.broadcasted_iota(jnp.int32, (rows, LANES), 1)
    low = lane < LOW
    zero = jnp.zeros((rows, LANES), packed.dtype)

    def one_irrep(g, start):
        extra = sizes_ref[con * own + g] - LOW
        tile = start // LANES
        shift = start - tile * LANES
        after = jnp.minimum(tile + 1, tiles - 1)
        tile = jnp.minimum(tile, tiles - 1)
        here = lane >= shift
        back = lax.rem(LANES - shift, LANES)
        back_half = lax.rem(LANES + LOW - shift, LANES)
        valid = lane < extra
        valid_half = jnp.where(low, lane + LOW, lane - LOW) < extra
        for p in range(pairs):
            at = pl.multiple_of((g * pairs + p) * LANES, LANES)
            both = packed[:, pl.ds(at, LANES)]
            halves = []
            for c in (2 * p, 2 * p + 1):
                one = packed[:, pl.ds(pl.multiple_of(base + (c * tiles + tile) * LANES, LANES), LANES)]
                two = packed[:, pl.ds(pl.multiple_of(base + (c * tiles + after) * LANES, LANES), LANES)]
                halves.append(jnp.where(here, one, two))
            first = jnp.where(valid_half, roll(halves[0], back_half), zero)
            second = jnp.where(valid, roll(halves[1], back), zero)
            to = pl.multiple_of((g * pairs + p) * 3 * LANES, LANES)
            values = (jnp.where(low, both, first), jnp.where(low, first, both), second)
            for i, place in enumerate(places):
                for t, value in enumerate(values):
                    a_ref[pl.ds(place, ROWS), pl.ds(to + t * LANES, LANES)] = value[
                        i * ROWS : (i + 1) * ROWS
                    ]
        return start + extra

    start = jnp.int32(0)
    for g in range(own):
        start = start + jnp.where(con > 0, sizes_ref[g] - LOW, 0)
    lax.fori_loop(0, own, one_irrep, start)


PLANE = 4 * 2 * ROWS
SMEM = pl.BlockSpec(memory_space=pltpu.SMEM)
VMEM = pl.BlockSpec(memory_space=pltpu.VMEM)
HBM = pl.BlockSpec(memory_space=pltpu.HBM)
ANY = pl.BlockSpec(memory_space=pl.ANY)


def fetch(con, width, pieces, packed_ref, sems):
    depth = pieces[0].shape[0]
    copies = []
    for n, piece in enumerate(pieces):
        rows = pl.ds(n * depth, depth)
        copies += [
            pltpu.make_async_copy(
                piece.at[:, pl.ds(pl.multiple_of(con * width, LANES), width)],
                packed_ref.at[rows, pl.ds(0, width)],
                sems.at[n, 0],
            ),
            pltpu.make_async_copy(
                piece.at[:, pl.ds(2 * width, 2 * width)],
                packed_ref.at[rows, pl.ds(width, 2 * width)],
                sems.at[n, 1],
            ),
        ]
    return copies


def places_in_plane(chip, con):
    inside = chip % 4
    places = []
    for core in (con, 1 - con):
        for c in (inside, inside ^ (1 + core), inside ^ (2 - core), inside ^ 3):
            places.append((c * 2 + core) * ROWS)
    return places


def unpack_kernel(cw, nirrep, numbers_ref, *refs):
    pieces = refs[:4]
    a_ref, packed_ref, sems = refs[4:]
    chip, con = numbers_ref[nirrep], numbers_ref[nirrep + 1]
    copies = fetch(con, a_ref.shape[1] // 3, pieces, packed_ref, sems)
    for copy in copies:
        copy.start()
    for copy in copies:
        copy.wait()
    places = [pl.multiple_of(place, ROWS) for place in places_in_plane(chip, con)]
    unpack_rows(cw, nirrep, numbers_ref, con, packed_ref, places, a_ref)


def unpack(numbers, pieces, cw, nirrep, flops):
    k = nirrep // 2 * cw * DMAX
    return pl.pallas_call(
        functools.partial(unpack_kernel, cw, nirrep),
        out_shape=pltpu.VMEM((PLANE, k), jnp.bfloat16),
        in_specs=[SMEM] + [ANY] * 4,
        out_specs=VMEM,
        scratch_shapes=[
            pltpu.VMEM((PLANE, k), jnp.bfloat16),
            pltpu.SemaphoreType.DMA((4, 2)),
        ],
        compiler_params=pltpu.CompilerParams(vmem_limit_bytes=44 * 2**20),
        cost_estimate=pl.CostEstimate(flops=flops, bytes_accessed=4 * PLANE * k, transcendentals=0),
        name="unpack",
    )(numbers, *pieces)


def contract_kernel(cw, nirrep, ready, packed, numbers_ref, *refs):
    chip, con = numbers_ref[nirrep], numbers_ref[nirrep + 1]
    z = chip // 4
    rows_ready, pieces = refs[: len(ready)], refs[len(ready) : len(ready) + 4 * len(packed)]
    refs = refs[len(ready) + 4 * len(packed) :]
    w_hbm, keep_ref, send_out, a_ref, w_ref, packed_ref, send_ref, sems, w_sems, out_sems = refs
    block = w_ref.shape[0] // w_sems.shape[0]
    half = send_ref.shape[0]
    total = 2 * half
    width = w_ref.shape[1] // 3
    before = jnp.where(z == 0, 2, jnp.where(z == 1, 0, jnp.where(z == 2, 3, 1)))
    planes = {0: z, 1: before, 3: 3 - before, 2: 3 - z}

    def start_of(plane):
        return pl.multiple_of(lax.rem(plane * PLANE + total - con * half, total), PLANE)

    copies = []
    for n in range(len(packed)):
        copies += fetch(con, width, pieces[4 * n : 4 * n + 4], packed_ref.at[n], sems.at[n])
    w_copies = [
        pltpu.make_async_copy(
            w_hbm.at[pl.ds(n * block, block)], w_ref.at[pl.ds(n * block, block)], w_sems.at[n]
        )
        for n in range(w_sems.shape[0])
    ]
    for copy in copies + w_copies:
        copy.start()
    inner = places_in_plane(chip, con)
    for k, rows in zip(ready, rows_ready):
        a_ref[pl.ds(start_of(planes[k]), PLANE)] = rows[...]

    @pl.loop(0, len(packed))
    def _(n):
        plane = planes[packed[0]]
        for i, k in enumerate(packed[1:]):
            plane = jnp.where(n == i + 1, planes[k], plane)
        places = [pl.multiple_of(start_of(plane) + place, ROWS) for place in inner]
        for copy in fetch(con, width, pieces[:4], packed_ref.at[n], sems.at[n]):
            copy.wait()
        unpack_rows(cw, nirrep, numbers_ref, con, packed_ref.at[n], places, a_ref)

    def send_copy(n):
        columns = pl.ds(pl.multiple_of(n * block, block), block)
        return pltpu.make_async_copy(
            send_ref.at[:, columns], send_out.at[:, columns], out_sems.at[n]
        )

    @pl.loop(0, w_sems.shape[0])
    def _(n):
        columns = pl.ds(pl.multiple_of(n * block, block), block)
        pltpu.make_async_copy(w_ref.at[columns], w_ref.at[columns], w_sems.at[n]).wait()
        sums = lax.dot_general(
            a_ref[...],
            w_ref[columns, :],
            (((1,), (1,)), ((), ())),
            preferred_element_type=jnp.float32,
        )
        keep_ref[:, columns] = sums[:half]
        send_ref[:, columns] = sums[half:]
        send_copy(n).start()

    @pl.loop(0, w_sems.shape[0])
    def _(n):
        send_copy(n).wait()


def contract(numbers, ready, packed, integrals, cw, nirrep):
    n, k = integrals.shape
    total = PLANE * (len(ready) + len(packed))
    half = jax.ShapeDtypeStruct((total // 2, n), jnp.float32)
    pieces = [piece for plane in packed.values() for piece in plane]
    return pl.pallas_call(
        functools.partial(contract_kernel, cw, nirrep, tuple(ready), tuple(packed)),
        out_shape=(pltpu.VMEM(half.shape, half.dtype), half),
        in_specs=[SMEM] + [VMEM] * len(ready) + [ANY] * len(pieces) + [HBM],
        out_specs=(VMEM, HBM),
        scratch_shapes=[
            pltpu.VMEM((total, k), jnp.bfloat16),
            pltpu.VMEM((n, k), jnp.bfloat16),
            pltpu.VMEM((len(packed), PLANE, k), jnp.bfloat16),
            pltpu.VMEM((total // 2, n), jnp.float32),
            pltpu.SemaphoreType.DMA((len(packed), 4, 2)),
            pltpu.SemaphoreType.DMA((n // 256,)),
            pltpu.SemaphoreType.DMA((n // 256,)),
        ],
        compiler_params=pltpu.CompilerParams(vmem_limit_bytes=44 * 2**20),
        name="contract",
    )(
        numbers,
        *(pltpu.with_memory_space_constraint(rows, pltpu.VMEM) for rows in ready.values()),
        *pieces,
        integrals,
    )


def add_kernel(keep_ref, got_ref, out, out_ref, sems):
    parts = sems.shape[0]
    rows = out_ref.shape[0] // parts

    def copy_out(n):
        part = pl.ds(pl.multiple_of(n * rows, rows), rows)
        return pltpu.make_async_copy(out_ref.at[part], out.at[part], sems.at[n])

    @pl.loop(0, parts)
    def _(n):
        part = pl.ds(pl.multiple_of(n * rows, rows), rows)
        out_ref[part] = (keep_ref[part] + got_ref[part]).astype(out_ref.dtype)
        copy_out(n).start()

    @pl.loop(0, parts)
    def _(n):
        copy_out(n).wait()


def add(keep, got):
    keep, got = (pltpu.with_memory_space_constraint(x, pltpu.VMEM) for x in (keep, got))
    return pl.pallas_call(
        add_kernel,
        out_shape=jax.ShapeDtypeStruct(keep.shape, jnp.bfloat16),
        in_specs=[VMEM, VMEM],
        out_specs=HBM,
        scratch_shapes=[pltpu.VMEM(keep.shape, jnp.bfloat16), pltpu.SemaphoreType.DMA((4,))],
        compiler_params=pltpu.CompilerParams(vmem_limit_bytes=4 * 2**20),
        name="add",
    )(keep, got)


RING = (1, 3, 0, 2)
RING_BACK = (2, 0, 3, 1)


def x_neighbour(o):
    return o ^ 1


def y_neighbour(o):
    return o ^ 2


def z_next(o):
    return RING[o // 4] * 4 + o % 4


def z_previous(o):
    return RING_BACK[o // 4] * 4 + o % 4


def after(value, *others):
    return lax.optimization_barrier((value, *others))[0]


STEPS = {
    "z1": (("own",), "next"),
    "f0": (("own",), "first"),
    "z3": (("own",), "previous"),
    "s0": (("own", "f0"), "second"),
    "z2": (("z1",), "next"),
    "f1": (("z1",), "first"),
    "f3": (("z3",), "first"),
    "s1": (("s0",), "next"),
    "f2": (("z2",), "first"),
    "s3": (("z3", "f3"), "second"),
    "s2": (("z2", "f2"), "second"),
}
AFTER = {"z3": ("f0",), "f3": ("s0",), "f2": ("f1",)}
READY = {0: 10**9}
LATE = (1,)


def ladder_of_16(amplitudes, integrals, block_sizes):
    out_count, con_count = lax.axis_size("out"), lax.axis_size("con")
    ways = {
        "next": (z_next,),
        "previous": (z_previous,),
        "first": (x_neighbour, y_neighbour),
        "second": (y_neighbour, x_neighbour),
    }

    def move(value, way):
        by_core = ways[way]
        pairs = [
            (o * con_count + c, by_core[c % len(by_core)](o) * con_count + c)
            for o in range(out_count)
            for c in range(con_count)
        ]
        return lax.ppermute(value, ("out", "con"), pairs)

    def swap_cores(value):
        return lax.ppermute(value, "con", [(0, 1), (1, 0)])

    cw = integrals.shape[1] // (block_sizes.shape[0] // con_count * DMAX)
    here = jnp.stack([lax.axis_index("out"), lax.axis_index("con")]).astype(jnp.int32)
    numbers = jnp.concatenate([block_sizes, here])
    own, own_top = pack(amplitudes, block_sizes, cw)
    arrays = {("own",): own}

    def get(names):
        if names not in arrays:
            one, two = (arrays[(name,)] for name in names)
            if names[0] == "own":
                arrays[names] = lax.dynamic_update_slice(own_top, two, (ROWS, 0))
            else:
                arrays[names] = jnp.concatenate([one, two])
        return arrays[names]

    steps = dict(STEPS)
    while steps:
        name = next(
            n
            for n, (sent, _) in steps.items()
            if all((o,) in arrays for o in sent + AFTER.get(n, ()))
        )
        sent, way = steps.pop(name)
        others = [arrays[(o,)] for o in AFTER.get(name, ())]
        if name == "z2":
            others.append(numbers)
        value = get(sent)
        arrays[(name,)] = move(after(value, *others) if others else value, way)

    nirrep = block_sizes.shape[0]
    ready, packed = {}, {}
    for k, z in ((0, "own"), (2, "z2"), (1, "z1"), (3, "z3")):
        last = arrays[(f"s{k}",)]
        if k in LATE:
            last = after(last, *ready.values())
        plane = [get((z, f"f{k}")), last]
        plane += [swap_cores(piece) for piece in plane]
        if k in READY:
            ready[k] = unpack(numbers, plane, cw, nirrep, READY[k])
        else:
            packed[k] = plane
    keep, send = contract(numbers, ready, packed, integrals, cw, nirrep)
    return add(keep, swap_cores(send))


def on_device(amplitudes, integrals, block_sizes):
    if amplitudes.shape[0] == ROWS and lax.axis_size("out") == 16:
        return ladder_of_16(amplitudes, integrals, block_sizes)
    return general(amplitudes, integrals, block_sizes)


def solution(mesh):
    in_specs = (P(("out", "con"), None), P("out", "con"), P())
    out_specs = P("con", "out")
    return jax.shard_map(
        on_device, mesh=mesh, in_specs=in_specs, out_specs=out_specs, check_vma=False
    )
```

```python
import functools

import jax
import jax.numpy as jnp
from jax import lax
from jax.experimental import pallas as pl
from jax.experimental.pallas import tpu as pltpu
from jax.sharding import PartitionSpec as P

DMAX = 192
LANES = 128
LOW = 64
ROWS = 16


def mask_slots(amplitudes, block_sizes):
    row_count = amplitudes.shape[0]
    nirrep = block_sizes.shape[0]
    blocked = amplitudes.reshape(row_count, nirrep, -1, DMAX)
    valid_cols = jnp.arange(DMAX, dtype=jnp.int32)[None, :] < block_sizes[:, None]
    masked = jnp.where(valid_cols[None, :, None, :], blocked, jnp.zeros((), amplitudes.dtype))
    return masked.reshape(row_count, -1)


def general(amplitudes, integrals, block_sizes):
    masked = mask_slots(amplitudes, block_sizes)
    gathered = lax.all_gather(masked, "out", axis=0, tiled=True)
    own_columns = lax.all_to_all(gathered, "con", split_axis=1, concat_axis=0, tiled=True)
    out_count = lax.axis_size("out")
    con_count = lax.axis_size("con")
    per_device = masked.shape[0]
    own_columns = own_columns.reshape(con_count, out_count, per_device, -1)
    own_columns = jnp.transpose(own_columns, (1, 0, 2, 3)).reshape(
        con_count * out_count * per_device, -1
    )
    partial_sums = lax.dot_general(
        own_columns, integrals, (((1,), (1,)), ((), ())), preferred_element_type=jnp.float32
    )
    ladder = lax.psum_scatter(partial_sums, "con", scatter_dimension=0, tiled=True)
    return ladder.astype(jnp.bfloat16)


def roll(x, shift):
    return pltpu.roll(x, shift, 1)


def pack_kernel(nirrep, cw, sizes_ref, amp_ref, out_ref, both_ref):
    pairs = cw // 2
    rows = amp_ref.shape[0]
    lane = lax.broadcasted_iota(jnp.int32, (rows, LANES), 1)
    low = lane < LOW
    tiles = nirrep // 2
    extras = [[jnp.zeros((rows, LANES), amp_ref.dtype)] * tiles for _ in range(cw)]
    start = jnp.int32(0)
    for g in range(nirrep):
        extra = sizes_ref[g] - LOW
        inside = [
            (lane + k * LANES >= start) & (lane + k * LANES < start + extra) for k in range(tiles)
        ]
        shift = lax.rem(start, LANES)
        shift_half = lax.rem(start + LOW, LANES)
        for p in range(pairs):
            at = (g * pairs + p) * 3 * LANES
            one = amp_ref[:, at : at + LANES]
            two = amp_ref[:, at + LANES : at + 2 * LANES]
            three = amp_ref[:, at + 2 * LANES : at + 3 * LANES]
            to = (g * pairs + p) * LANES
            value = jnp.where(low, one, two)
            out_ref[:, to : to + LANES] = value
            both_ref[:rows, to : to + LANES] = value
            first = roll(jnp.where(low, two, one), shift_half)
            second = roll(three, shift)
            for k in range(tiles):
                extras[2 * p][k] = jnp.where(inside[k], first, extras[2 * p][k])
                extras[2 * p + 1][k] = jnp.where(inside[k], second, extras[2 * p + 1][k])
        start = start + extra
    base = nirrep * pairs * LANES
    for c in range(cw):
        for k in range(tiles):
            to = base + (c * tiles + k) * LANES
            out_ref[:, to : to + LANES] = extras[c][k]
            both_ref[:rows, to : to + LANES] = extras[c][k]


def pack(amplitudes, block_sizes, cw):
    nirrep = block_sizes.shape[0]
    rows, dtype = amplitudes.shape[0], amplitudes.dtype
    return pl.pallas_call(
        functools.partial(pack_kernel, nirrep, cw),
        out_shape=(
            jax.ShapeDtypeStruct((rows, nirrep * cw * LANES), dtype),
            pltpu.VMEM((2 * rows, nirrep * cw * LANES), dtype),
        ),
        in_specs=[
            pl.BlockSpec(memory_space=pltpu.SMEM),
            pl.BlockSpec(memory_space=pltpu.VMEM),
        ],
        out_specs=(
            pl.BlockSpec(memory_space=pltpu.VMEM),
            pl.BlockSpec(memory_space=pltpu.VMEM),
        ),
        compiler_params=pltpu.CompilerParams(vmem_limit_bytes=48 * 2**20),
        name="pack",
    )(block_sizes, amplitudes)


def unpack_rows(cw, nirrep, sizes_ref, con, packed, places, a_ref):
    pairs = cw // 2
    tiles = nirrep // 2
    own = nirrep // 2
    base = own * pairs * LANES
    rows = packed.shape[0]
    lane = lax.broadcasted_iota(jnp.int32, (rows, LANES), 1)
    low = lane < LOW
    zero = jnp.zeros((rows, LANES), packed.dtype)

    def one_irrep(g, start):
        extra = sizes_ref[con * own + g] - LOW
        tile = start // LANES
        shift = start - tile * LANES
        after = jnp.minimum(tile + 1, tiles - 1)
        tile = jnp.minimum(tile, tiles - 1)
        here = lane >= shift
        back = lax.rem(LANES - shift, LANES)
        back_half = lax.rem(LANES + LOW - shift, LANES)
        valid = lane < extra
        valid_half = jnp.where(low, lane + LOW, lane - LOW) < extra
        for p in range(pairs):
            at = pl.multiple_of((g * pairs + p) * LANES, LANES)
            both = packed[:, pl.ds(at, LANES)]
            halves = []
            for c in (2 * p, 2 * p + 1):
                one = packed[:, pl.ds(pl.multiple_of(base + (c * tiles + tile) * LANES, LANES), LANES)]
                two = packed[:, pl.ds(pl.multiple_of(base + (c * tiles + after) * LANES, LANES), LANES)]
                halves.append(jnp.where(here, one, two))
            first = jnp.where(valid_half, roll(halves[0], back_half), zero)
            second = jnp.where(valid, roll(halves[1], back), zero)
            to = pl.multiple_of((g * pairs + p) * 3 * LANES, LANES)
            values = (jnp.where(low, both, first), jnp.where(low, first, both), second)
            for i, place in enumerate(places):
                for t, value in enumerate(values):
                    a_ref[pl.ds(place, ROWS), pl.ds(to + t * LANES, LANES)] = value[
                        i * ROWS : (i + 1) * ROWS
                    ]
        return start + extra

    start = jnp.int32(0)
    for g in range(own):
        start = start + jnp.where(con > 0, sizes_ref[g] - LOW, 0)
    lax.fori_loop(0, own, one_irrep, start)


PLANE = 4 * 2 * ROWS
SMEM = pl.BlockSpec(memory_space=pltpu.SMEM)
VMEM = pl.BlockSpec(memory_space=pltpu.VMEM)
HBM = pl.BlockSpec(memory_space=pltpu.HBM)
ANY = pl.BlockSpec(memory_space=pl.ANY)


def fetch(con, width, pieces, packed_ref, sems):
    depth = pieces[0].shape[0]
    copies = []
    for n, piece in enumerate(pieces):
        rows = pl.ds(n * depth, depth)
        copies += [
            pltpu.make_async_copy(
                piece.at[:, pl.ds(pl.multiple_of(con * width, LANES), width)],
                packed_ref.at[rows, pl.ds(0, width)],
                sems.at[n, 0],
            ),
            pltpu.make_async_copy(
                piece.at[:, pl.ds(2 * width, 2 * width)],
                packed_ref.at[rows, pl.ds(width, 2 * width)],
                sems.at[n, 1],
            ),
        ]
    return copies


def places_in_plane(chip, con):
    inside = chip % 4
    places = []
    for core in (con, 1 - con):
        for c in (inside, inside ^ (1 + core), inside ^ (2 - core), inside ^ 3):
            places.append((c * 2 + core) * ROWS)
    return places


def unpack_kernel(cw, nirrep, numbers_ref, *refs):
    pieces = refs[:4]
    a_ref, packed_ref, sems = refs[4:]
    chip, con = numbers_ref[nirrep], numbers_ref[nirrep + 1]
    copies = fetch(con, a_ref.shape[1] // 3, pieces, packed_ref, sems)
    for copy in copies:
        copy.start()
    for copy in copies:
        copy.wait()
    places = [pl.multiple_of(place, ROWS) for place in places_in_plane(chip, con)]
    unpack_rows(cw, nirrep, numbers_ref, con, packed_ref, places, a_ref)


def unpack(numbers, pieces, cw, nirrep, flops):
    k = nirrep // 2 * cw * DMAX
    return pl.pallas_call(
        functools.partial(unpack_kernel, cw, nirrep),
        out_shape=pltpu.VMEM((PLANE, k), jnp.bfloat16),
        in_specs=[SMEM] + [ANY] * 4,
        out_specs=VMEM,
        scratch_shapes=[
            pltpu.VMEM((PLANE, k), jnp.bfloat16),
            pltpu.SemaphoreType.DMA((4, 2)),
        ],
        compiler_params=pltpu.CompilerParams(vmem_limit_bytes=44 * 2**20),
        cost_estimate=pl.CostEstimate(flops=flops, bytes_accessed=4 * PLANE * k, transcendentals=0),
        name="unpack",
    )(numbers, *pieces)


def contract_kernel(cw, nirrep, ready, packed, numbers_ref, *refs):
    chip, con = numbers_ref[nirrep], numbers_ref[nirrep + 1]
    z = chip // 4
    rows_ready, pieces = refs[: len(ready)], refs[len(ready) : len(ready) + 4 * len(packed)]
    refs = refs[len(ready) + 4 * len(packed) :]
    w_hbm, keep_ref, send_out, a_ref, w_ref, packed_ref, send_ref, sems, w_sems, out_sems = refs
    block = w_ref.shape[0] // w_sems.shape[0]
    half = send_ref.shape[0]
    total = 2 * half
    width = w_ref.shape[1] // 3
    before = jnp.where(z == 0, 2, jnp.where(z == 1, 0, jnp.where(z == 2, 3, 1)))
    planes = {0: z, 1: before, 3: 3 - before, 2: 3 - z}

    def start_of(plane):
        return pl.multiple_of(lax.rem(plane * PLANE + total - con * half, total), PLANE)

    copies = []
    for n in range(len(packed)):
        copies += fetch(con, width, pieces[4 * n : 4 * n + 4], packed_ref.at[n], sems.at[n])
    w_copies = [
        pltpu.make_async_copy(
            w_hbm.at[pl.ds(n * block, block)], w_ref.at[pl.ds(n * block, block)], w_sems.at[n]
        )
        for n in range(w_sems.shape[0])
    ]
    for copy in copies + w_copies:
        copy.start()
    inner = places_in_plane(chip, con)
    for k, rows in zip(ready, rows_ready):
        a_ref[pl.ds(start_of(planes[k]), PLANE)] = rows[...]

    @pl.loop(0, len(packed))
    def _(n):
        plane = planes[packed[0]]
        for i, k in enumerate(packed[1:]):
            plane = jnp.where(n == i + 1, planes[k], plane)
        places = [pl.multiple_of(start_of(plane) + place, ROWS) for place in inner]
        for copy in fetch(con, width, pieces[:4], packed_ref.at[n], sems.at[n]):
            copy.wait()
        unpack_rows(cw, nirrep, numbers_ref, con, packed_ref.at[n], places, a_ref)

    def send_copy(n):
        columns = pl.ds(pl.multiple_of(n * block, block), block)
        return pltpu.make_async_copy(
            send_ref.at[:, columns], send_out.at[:, columns], out_sems.at[n]
        )

    @pl.loop(0, w_sems.shape[0])
    def _(n):
        columns = pl.ds(pl.multiple_of(n * block, block), block)
        pltpu.make_async_copy(w_ref.at[columns], w_ref.at[columns], w_sems.at[n]).wait()
        sums = lax.dot_general(
            a_ref[...],
            w_ref[columns, :],
            (((1,), (1,)), ((), ())),
            preferred_element_type=jnp.float32,
        )
        keep_ref[:, columns] = sums[:half]
        send_ref[:, columns] = sums[half:]
        send_copy(n).start()

    @pl.loop(0, w_sems.shape[0])
    def _(n):
        send_copy(n).wait()


def contract(numbers, ready, packed, integrals, cw, nirrep):
    n, k = integrals.shape
    total = PLANE * (len(ready) + len(packed))
    half = jax.ShapeDtypeStruct((total // 2, n), jnp.float32)
    pieces = [piece for plane in packed.values() for piece in plane]
    return pl.pallas_call(
        functools.partial(contract_kernel, cw, nirrep, tuple(ready), tuple(packed)),
        out_shape=(pltpu.VMEM(half.shape, half.dtype), half),
        in_specs=[SMEM] + [VMEM] * len(ready) + [ANY] * len(pieces) + [HBM],
        out_specs=(VMEM, HBM),
        scratch_shapes=[
            pltpu.VMEM((total, k), jnp.bfloat16),
            pltpu.VMEM((n, k), jnp.bfloat16),
            pltpu.VMEM((len(packed), PLANE, k), jnp.bfloat16),
            pltpu.VMEM((total // 2, n), jnp.float32),
            pltpu.SemaphoreType.DMA((len(packed), 4, 2)),
            pltpu.SemaphoreType.DMA((n // 256,)),
            pltpu.SemaphoreType.DMA((n // 256,)),
        ],
        compiler_params=pltpu.CompilerParams(vmem_limit_bytes=44 * 2**20),
        name="contract",
    )(
        numbers,
        *(pltpu.with_memory_space_constraint(rows, pltpu.VMEM) for rows in ready.values()),
        *pieces,
        integrals,
    )


def add_kernel(keep_ref, got_ref, out, out_ref, sems):
    parts = sems.shape[0]
    rows = out_ref.shape[0] // parts

    def copy_out(n):
        part = pl.ds(pl.multiple_of(n * rows, rows), rows)
        return pltpu.make_async_copy(out_ref.at[part], out.at[part], sems.at[n])

    @pl.loop(0, parts)
    def _(n):
        part = pl.ds(pl.multiple_of(n * rows, rows), rows)
        out_ref[part] = (keep_ref[part] + got_ref[part]).astype(out_ref.dtype)
        copy_out(n).start()

    @pl.loop(0, parts)
    def _(n):
        copy_out(n).wait()


def add(keep, got):
    keep, got = (pltpu.with_memory_space_constraint(x, pltpu.VMEM) for x in (keep, got))
    return pl.pallas_call(
        add_kernel,
        out_shape=jax.ShapeDtypeStruct(keep.shape, jnp.bfloat16),
        in_specs=[VMEM, VMEM],
        out_specs=HBM,
        scratch_shapes=[pltpu.VMEM(keep.shape, jnp.bfloat16), pltpu.SemaphoreType.DMA((4,))],
        compiler_params=pltpu.CompilerParams(vmem_limit_bytes=4 * 2**20),
        name="add",
    )(keep, got)


RING = (1, 3, 0, 2)
RING_BACK = (2, 0, 3, 1)


def x_neighbour(o):
    return o ^ 1


def y_neighbour(o):
    return o ^ 2


def z_next(o):
    return RING[o // 4] * 4 + o % 4


def z_previous(o):
    return RING_BACK[o // 4] * 4 + o % 4


def after(value, *others):
    return lax.optimization_barrier((value, *others))[0]


STEPS = {
    "z1": (("own",), "next"),
    "f0": (("own",), "first"),
    "z3": (("own",), "previous"),
    "s0": (("own", "f0"), "second"),
    "z2": (("z1",), "next"),
    "f1": (("z1",), "first"),
    "f3": (("z3",), "first"),
    "s1": (("s0",), "next"),
    "f2": (("z2",), "first"),
    "s3": (("z3", "f3"), "second"),
    "s2": (("z2", "f2"), "second"),
}
AFTER = {"z3": ("f0",), "f3": ("s0",), "f2": ("f1",)}
READY = {0: 10**9}
LATE = (1,)


def ladder_of_16(amplitudes, integrals, block_sizes):
    out_count, con_count = lax.axis_size("out"), lax.axis_size("con")
    ways = {
        "next": (z_next,),
        "previous": (z_previous,),
        "first": (x_neighbour, y_neighbour),
        "second": (y_neighbour, x_neighbour),
    }

    def move(value, way):
        by_core = ways[way]
        pairs = [
            (o * con_count + c, by_core[c % len(by_core)](o) * con_count + c)
            for o in range(out_count)
            for c in range(con_count)
        ]
        return lax.ppermute(value, ("out", "con"), pairs)

    def swap_cores(value):
        return lax.ppermute(value, "con", [(0, 1), (1, 0)])

    cw = integrals.shape[1] // (block_sizes.shape[0] // con_count * DMAX)
    here = jnp.stack([lax.axis_index("out"), lax.axis_index("con")]).astype(jnp.int32)
    numbers = jnp.concatenate([block_sizes, here])
    own, own_top = pack(amplitudes, block_sizes, cw)
    arrays = {("own",): own}

    def get(names):
        if names not in arrays:
            one, two = (arrays[(name,)] for name in names)
            if names[0] == "own":
                arrays[names] = lax.dynamic_update_slice(own_top, two, (ROWS, 0))
            else:
                arrays[names] = jnp.concatenate([one, two])
        return arrays[names]

    steps = dict(STEPS)
    while steps:
        name = next(
            n
            for n, (sent, _) in steps.items()
            if all((o,) in arrays for o in sent + AFTER.get(n, ()))
        )
        sent, way = steps.pop(name)
        others = [arrays[(o,)] for o in AFTER.get(name, ())]
        if name == "z2":
            others.append(numbers)
        value = get(sent)
        arrays[(name,)] = move(after(value, *others) if others else value, way)

    nirrep = block_sizes.shape[0]
    ready, packed = {}, {}
    for k, z in ((0, "own"), (2, "z2"), (1, "z1"), (3, "z3")):
        last = arrays[(f"s{k}",)]
        if k in LATE:
            last = after(last, *ready.values())
        plane = [get((z, f"f{k}")), last]
        plane += [swap_cores(piece) for piece in plane]
        if k in READY:
            ready[k] = unpack(numbers, plane, cw, nirrep, READY[k])
        else:
            packed[k] = plane
    keep, send = contract(numbers, ready, packed, integrals, cw, nirrep)
    return add(keep, swap_cores(send))


def on_device(amplitudes, integrals, block_sizes):
    if amplitudes.shape[0] == ROWS and lax.axis_size("out") == 16:
        return ladder_of_16(amplitudes, integrals, block_sizes)
    return general(amplitudes, integrals, block_sizes)


def solution(mesh):
    in_specs = (P(("out", "con"), None), P("out", "con"), P())
    out_specs = P("con", "out")
    return jax.shard_map(
        on_device, mesh=mesh, in_specs=in_specs, out_specs=out_specs, check_vma=False
    )
```
